32 devices in a mesh: row: 4 (over z), col: 8 (over y, x, core).
Axes of the slice: x: 2, y: 2, z: 4, core: 2. Of those that a mesh axis runs over, the one named last changes fastest.
Arguments:
- density: float32 [32, 256, 1024], P(None, 'row', 'col'), may hold values from -12 to 12
- active: int32 [4, 64], P('row', 'col'), may hold values from -1 to 7, as said below
- owner_map: int32 [4, 64], P('row', 'col'), may hold values from -1 to 7, as said below
- isovalues: float32 [3], replicated, may hold values from -0.6 to 0.6
Outputs:
- smoothed: float32 [32, 256, 1024], P(None, 'row', 'col')
- crossing: float32 [4, 24, 32768], P('row', 'col')
- normals: float32 [4, 24, 288], P('row', 'col')
The draws below stay inside these ranges and needn't reach their ends.
Inputs may be any that keep to these rules, and one draw needn't show every extreme that they name: `active`: each device lists distinct numbers of its own 8 bricks, followed by -1 to the end; in each mesh row one device lists all of its 8 bricks and every other device at most 4. `owner_map`: entry t names the mesh column, in the same mesh row, of the owner of the brick at entry t of active, and is -1 exactly where active is -1. At most 1 bricks of one device go to one owner, reached in every mesh row; the owners of a mesh row receive counts that differ by at most one, at most 3, reached in every mesh row.
All inputs are finite; a program needn't handle non-finite values.
Results may differ from the reference program's by a relative error of at most 0.0003.
Values sent between devices are 32-bit elements; how exact they have to be, the bound alone decides.
A program may use at most 256 MiB of HBM per device.

```python
import jax
import jax.numpy as jnp
from jax import lax

BRICK = 32
DEPTH = 32
BRICKS_X = 4
BRICKS_Y = 2
LEVELS = 3
OWN = 3
NX = 1024
NY = 256
N_ROW = 4
N_COL = 8


def routing_layout(key):
    col_count = NX // (BRICKS_X * BRICK)
    row_count = NY // (BRICKS_Y * BRICK)
    local_count = BRICKS_X * BRICKS_Y
    quarter = local_count // 4
    row_keys = jax.random.split(jax.random.fold_in(key, 11), row_count)

    def shuffle_one(brick_key):
        return jax.random.permutation(brick_key, local_count).astype(jnp.int32)

    def one_row(row_key):
        key_order, key_size, key_pick, key_owner = jax.random.split(row_key, 4)
        device_order = jax.random.permutation(key_order, col_count).astype(jnp.int32)
        drawn_sizes = jax.random.randint(key_size, (col_count,), 0, 2 * quarter + 1).astype(jnp.int32)
        places = jnp.arange(col_count, dtype=jnp.int32)
        opens_pair = places % 2 == 1
        unpaired = opens_pair & (places + 1 >= col_count)
        partner = jnp.concatenate([drawn_sizes[:1], drawn_sizes[:-1]])
        by_place = jnp.where(opens_pair, jnp.where(unpaired, quarter, drawn_sizes), 2 * quarter - partner)
        by_place = jnp.where(places == 0, local_count, by_place).astype(jnp.int32)
        counts = jnp.zeros((col_count,), jnp.int32).at[device_order].set(by_place)
        shuffled = jax.vmap(shuffle_one)(jax.random.split(key_pick, col_count))
        positions = jnp.arange(local_count, dtype=jnp.int32)
        is_live = positions[None, :] < counts[:, None]
        listed = jnp.where(is_live, shuffled, -1)
        starts = jnp.cumsum(counts, dtype=jnp.int32) - counts
        ranking = starts[:, None] + positions[None, :]
        owner_order = jax.random.permutation(key_owner, col_count).astype(jnp.int32)
        targets = jnp.where(is_live, owner_order[ranking % col_count], -1)
        return (listed.reshape(-1).astype(jnp.int32), targets.reshape(-1).astype(jnp.int32))
    return jax.vmap(one_row)(row_keys)


def draw_active(key, part):
    return routing_layout(key)[0]


def draw_owner_map(key, part):
    return routing_layout(key)[1]


def block_levels(rng, dims, shards, least, top_value):
    gain = 1.0
    for position, parts in shards:
        steps = jax.random.uniform(jax.random.fold_in(jax.random.fold_in(rng, 6), position), (parts,), jnp.float32, least / len(shards), top_value / len(shards))
        gain = gain * jnp.repeat(jnp.exp(steps), dims[position] // parts).reshape((-1,) + (1,) * (len(dims) - 1 - position))
    return gain


def centred(stream_key, shape, scale, reach, cuts=(), held_as=jnp.bfloat16):
    loudness = block_levels(stream_key, shape, cuts, -0.22, 0.18) if cuts else 1.0
    drawn = jax.random.normal(stream_key, shape, jnp.float32) * scale * loudness
    return jnp.minimum(jnp.maximum(drawn, -reach), reach).astype(held_as)


def setup_inputs(seed: int = 0) -> dict:
    key_of = jax.random.split(jax.random.key(seed), 5)
    density = centred(key_of[0], (DEPTH, NY, NX), 2.0, 12.0, ((1, 4), (2, 8)), jnp.float32)
    active = draw_active(jax.random.fold_in(key_of[4], 71), 0)
    owner_map = draw_owner_map(jax.random.fold_in(key_of[4], 71), 0)
    isovalues = jnp.clip(jax.random.uniform(key_of[3], (LEVELS,), jnp.float32, -0.6, 0.6), -0.6, 0.6)
    return dict(density=density, active=active, owner_map=owner_map, isovalues=isovalues)


def filter_valid(values, along):
    length = values.shape[along] - 4
    shifted = [lax.slice_in_dim(values, offset, offset + length, axis=along) for offset in range(5)]
    return (-shifted[0] + 4.0 * shifted[1] + 10.0 * shifted[2] + 4.0 * shifted[3] - shifted[4]) * 0.0625


def smooth(density):
    along_x = filter_valid(jnp.pad(density, ((0, 0), (0, 0), (2, 2))), 2)
    along_y = filter_valid(jnp.pad(along_x, ((0, 0), (2, 2), (0, 0))), 1)
    return filter_valid(jnp.pad(along_y, ((2, 2), (0, 0), (0, 0))), 0)


def brick_surface(brick_cells, isovalues):
    centre = brick_cells[1:-1, 1:-1, 1:-1]
    gradients = [
        (brick_cells[2:, 1:-1, 1:-1] - brick_cells[:-2, 1:-1, 1:-1]) * 0.5,
        (brick_cells[1:-1, 2:, 1:-1] - brick_cells[1:-1, :-2, 1:-1]) * 0.5,
        (brick_cells[1:-1, 1:-1, 2:] - brick_cells[1:-1, 1:-1, :-2]) * 0.5,
    ]
    base_cells = (slice(1, DEPTH + 1), slice(1, BRICK + 1), slice(1, BRICK + 1))
    next_cells = [
        (slice(2, DEPTH + 2), slice(1, BRICK + 1), slice(1, BRICK + 1)),
        (slice(1, DEPTH + 1), slice(2, BRICK + 2), slice(1, BRICK + 1)),
        (slice(1, DEPTH + 1), slice(1, BRICK + 1), slice(2, BRICK + 2)),
    ]
    crossing = jnp.zeros((DEPTH, BRICK, BRICK), jnp.float32)
    moments = [jnp.zeros((DEPTH,), jnp.float32)] * (LEVELS * 3)
    here = centre[base_cells]
    for ahead in next_cells:
        there = centre[ahead]
        for level_id in range(LEVELS):
            lower_gap = here - isovalues[level_id]
            upper_gap = there - isovalues[level_id]
            weight = jnp.maximum(0.0, -lower_gap * upper_gap)
            crossing = crossing + weight
            for component in range(3):
                moment_term = weight * (jnp.abs(upper_gap) * gradients[component][base_cells] + jnp.abs(lower_gap) * gradients[component][ahead])
                moments[level_id * 3 + component] = moments[level_id * 3 + component] + jnp.sum(moment_term, axis=(1, 2))
    normals = jnp.stack(moments, axis=0) * 0.0625
    return crossing.reshape(-1), normals.reshape(-1)


def reference(density, active, owner_map, isovalues):
    smoothed = smooth(density)
    padded = jnp.pad(smoothed, 2)
    local_count = BRICKS_X * BRICKS_Y
    listed = active.reshape(N_ROW, N_COL, local_count)
    targets = owner_map.reshape(N_ROW, N_COL, local_count)
    is_listed = listed >= 0
    entry_ids = jnp.arange(local_count, dtype=jnp.int32)
    earlier = (entry_ids[None, None, None, :] < entry_ids[None, None, :, None]) & (targets[:, :, None, :] == targets[:, :, :, None]) & is_listed[:, :, None, :]
    repeats = jnp.sum(earlier.astype(jnp.int32), axis=3, dtype=jnp.int32)
    owner_ids = jnp.arange(N_COL, dtype=jnp.int32)
    sends = jnp.sum(((targets[..., None] == owner_ids) & is_listed[..., None]).astype(jnp.int32), axis=2, dtype=jnp.int32)
    before = jnp.cumsum(sends, axis=1, dtype=jnp.int32) - sends
    numbers = jnp.take_along_axis(before, jnp.maximum(targets, 0).astype(jnp.int32), axis=2) + repeats
    row_ids = jnp.arange(N_ROW, dtype=jnp.int32)[:, None, None]
    slot_total = N_ROW * N_COL * OWN
    destination = jnp.where(is_listed, row_ids * (N_COL * OWN) + targets * OWN + numbers, slot_total).astype(jnp.int32)
    source_ids = jnp.full((slot_total + 1,), -1, jnp.int32).at[destination.reshape(-1)].set(jnp.arange(N_ROW * N_COL * local_count, dtype=jnp.int32))
    flat_listed = listed.reshape(-1)

    def one_slot(entry_id):
        present = entry_id >= 0
        entry_safe = jnp.maximum(entry_id, 0).astype(jnp.int32)
        mesh_row = entry_safe // (N_COL * local_count)
        mesh_col = (entry_safe // local_count) % N_COL
        brick_id = jnp.maximum(flat_listed[entry_safe], 0).astype(jnp.int32)
        y_start = ((mesh_row * BRICKS_Y + brick_id // BRICKS_X) * BRICK).astype(jnp.int32)
        x_start = ((mesh_col * BRICKS_X + brick_id % BRICKS_X) * BRICK).astype(jnp.int32)
        brick_cells = lax.dynamic_slice(padded, (jnp.zeros((), jnp.int32), y_start, x_start), (DEPTH + 4, BRICK + 4, BRICK + 4))
        crossing, normals = brick_surface(brick_cells, isovalues)
        return jnp.where(present, crossing, 0.0), jnp.where(present, normals, 0.0)

    crossing, normals = lax.map(one_slot, source_ids[:slot_total])
    return smoothed, crossing.reshape(N_ROW, N_COL * OWN, DEPTH * BRICK * BRICK), normals.reshape(N_ROW, N_COL * OWN, LEVELS * 3 * DEPTH)
```

```python
import functools

import jax
import jax.numpy as jnp
from jax import lax
from jax.experimental import pallas as pl
from jax.experimental.pallas import tpu as pltpu
from jax.sharding import PartitionSpec as P

BRICK = 32
LEVELS = 3
LANES = 128
PAY = 264
CH = 8
MESH = pl.DeviceIdType.MESH
F32 = jnp.float32
DIRS = ((-1, 0), (1, 0), (0, -1), (0, 1), (-1, -1), (-1, 1), (1, -1), (1, 1))


def iota(shape, dim):
    return lax.broadcasted_iota(jnp.int32, shape, dim)


def five(far, near, mid):
    return 10.0 * mid + 4.0 * near - far


def kernel(
    rows_n, cols_n, dens, active, owner, iso,
    smooth, recv,
    dext, side_l, side_r, pack_l, pack_r, shifted, wmat, cells, bricks, nrm, acc, send,
    hs_send, hs_recv, a_send, a_recv,
):
    depth = dens.shape[0]
    height = dens.shape[1]
    ext = height + 16
    r = lax.axis_index("row")
    c = lax.axis_index("col")
    up, down = r > 0, r < rows_n - 1
    left, right = c > 0, c < cols_n - 1

    def exists(dy, dx):
        ok = None
        for d, lo, hi in ((dy, up, down), (dx, left, right)):
            if d:
                e = lo if d < 0 else hi
                ok = e if ok is None else jnp.logical_and(ok, e)
        return ok

    barrier = pltpu.get_barrier_semaphore()
    for dy, dx in DIRS:
        if dy:
            @pl.when(exists(dy, dx))
            def _():
                pl.semaphore_signal(barrier, inc=1, device_id=(r + dy, c + dx), device_id_type=MESH)
    for k in range(1, cols_n):
        pl.semaphore_signal(
            barrier, inc=1, device_id=(r, lax.rem(c + k, cols_n)), device_id_type=MESH
        )

    lane = iota((height, LANES), 1)
    group = lane // 4

    def pack(z, carry):
        first, last = carry
        rolled = pltpu.roll(dens[z], 4 * z, 1)
        first = jnp.where(group == z, rolled, first)
        last = jnp.where(group == (z + depth - 1) % depth, rolled, last)
        dext[z + 2, 8 : 8 + height, :] = dens[z]
        return first, last

    zero = jnp.zeros((height, LANES), F32)
    first, last = lax.fori_loop(0, depth, pack, (zero, zero))
    pack_l[...] = first
    pack_r[...] = last

    n_wait = (cols_n - 1) + (up.astype(jnp.int32) + down.astype(jnp.int32)) * (
        1 + left.astype(jnp.int32) + right.astype(jnp.int32)
    )
    pl.semaphore_wait(barrier, n_wait)

    top, body, bottom = pl.ds(0, 8), pl.ds(8, height), pl.ds(8 + height, 8)
    inner_top, inner_bottom = pl.ds(0, 8), pl.ds(height - 8, 8)
    layers = pl.ds(2, depth)
    plans = {
        (-1, 0): (dens.at[:, inner_top, :], dext.at[layers, bottom, :]),
        (1, 0): (dens.at[:, inner_bottom, :], dext.at[layers, top, :]),
        (0, -1): (pack_l, side_r.at[body, :]),
        (0, 1): (pack_r, side_l.at[body, :]),
        (-1, -1): (pack_l.at[inner_top, :], side_r.at[bottom, :]),
        (-1, 1): (pack_r.at[inner_top, :], side_l.at[bottom, :]),
        (1, -1): (pack_l.at[inner_bottom, :], side_r.at[top, :]),
        (1, 1): (pack_r.at[inner_bottom, :], side_l.at[top, :]),
    }
    halo = []
    for n, (dy, dx) in enumerate(DIRS):
        src, dst = plans[(dy, dx)]
        copy = pltpu.make_async_remote_copy(
            src_ref=src, dst_ref=dst, send_sem=hs_send.at[n], recv_sem=hs_recv.at[n],
            device_id=(r + dy, c + dx), device_id_type=MESH,
        )
        halo.append(copy)

        @pl.when(exists(dy, dx))
        def _():
            copy.start()

    for dy, dx in DIRS:
        @pl.when(jnp.logical_not(exists(-dy, -dx)))
        def _():
            dst = plans[(dy, dx)][1]
            dst[...] = jnp.zeros(dst.shape, F32)
    plane0 = jnp.zeros((ext, LANES), F32)
    for z in (0, 1, depth + 2, depth + 3):
        dext[z] = plane0
    for q in range(4):
        for z in (0, depth + 1, depth + 2):
            shifted[q, z] = plane0

    k_id = iota((2 * LANES, LANES), 0)
    n_id = iota((2 * LANES, LANES), 1)
    k_col = jnp.where(k_id < LANES + LANES // 2, k_id, k_id - 2 * LANES)
    for q in range(4):
        col = n_id + (q - 1)
        gap = jnp.abs(k_col - col)
        tap = jnp.where(gap == 0, 10.0, jnp.where(gap == 1, 4.0, jnp.where(gap == 2, -1.0, 0.0)))
        inside = ((col >= 0) | left) & ((col < LANES) | right)
        wmat[:, q * LANES : (q + 1) * LANES] = jnp.where(
            inside, tap * (1.0 / 4096.0), 0.0
        ).astype(jnp.bfloat16)
    for b in range(2):
        acc[b, LEVELS * 3 * depth * 8 :, :] = jnp.zeros(
            (acc.shape[1] - LEVELS * 3 * depth * 8, LANES), F32
        )

    for n, (dy, dx) in enumerate(DIRS):
        @pl.when(exists(-dy, -dx))
        def _():
            halo[n].wait_recv()
    for n, (dy, dx) in enumerate(DIRS):
        @pl.when(exists(dy, dx))
        def _():
            halo[n].wait_send()

    row_id = iota((ext, LANES), 0)
    lane_id = iota((ext, LANES), 1)
    in_rows = ((row_id >= 8) | up) & ((row_id < 8 + height) | down)

    def along_y(v):
        return five(
            pltpu.roll(v, 2, 0) + pltpu.roll(v, ext - 2, 0),
            pltpu.roll(v, 1, 0) + pltpu.roll(v, ext - 1, 0),
            v,
        )

    def side_filter(v):
        def moved(k):
            if k > 0:
                return jnp.where(lane_id < LANES - 4 * k, pltpu.roll(v, LANES - 4 * k, 1), 0.0)
            return jnp.where(lane_id >= -4 * k, pltpu.roll(v, -4 * k, 1), 0.0)

        out = along_y(five(moved(-2) + moved(2), moved(-1) + moved(1), v))
        return jnp.where(in_rows, out, 0.0)

    side_r[...] = side_filter(side_r[...])
    side_l[...] = pltpu.roll(side_filter(pltpu.roll(side_l[...], 4, 1)), LANES - 4, 1)

    def filtered(z, carry):
        v = [dext[z + i] for i in range(5)]
        main = along_y(five(v[0] + v[4], v[1] + v[3], v[2]))
        main = jnp.where(in_rows, main, 0.0)
        back = (LANES - 4 * z) % LANES
        edge = jnp.where(
            lane_id < 4,
            pltpu.roll(side_r[...], back, 1),
            jnp.where(lane_id >= LANES - 4, pltpu.roll(side_l[...], back, 1), 0.0),
        )
        both = jnp.concatenate([main, edge], axis=1)
        high = both.astype(jnp.bfloat16)
        low = (both - high.astype(F32)).astype(jnp.bfloat16)
        w = wmat[...]
        out = jnp.dot(high, w, preferred_element_type=F32) + jnp.dot(
            low, w, preferred_element_type=F32
        )
        for q in range(4):
            shifted[q, z + 1] = out[:, q * LANES : (q + 1) * LANES]
        smooth[z] = out[8 : 8 + height, LANES : 2 * LANES]
        return carry

    lax.fori_loop(0, depth, filtered, 0)

    levels = [iso[i] for i in range(LEVELS)]

    def layer(z):
        for half in range(2):
            sums = [jnp.zeros((8, LANES), F32)] * (LEVELS * 3)
            for strip in range(4):
                base = 8 + half * BRICK + strip * 8

                def at(q, dz=0, dy=0):
                    return shifted[q, z + 1 + dz, pl.ds(base + dy, 8), :]

                here, ahead_x = at(1), at(2)
                ahead_y, ahead_z = at(1, 0, 1), at(1, 1)
                back_z = at(1, -1)
                grads = (
                    (
                        ahead_z - back_z,
                        at(2, 1) - at(2, -1),
                        at(1, 1, 1) - at(1, -1, 1),
                        at(1, 2) - here,
                    ),
                    (
                        ahead_y - at(1, 0, -1),
                        at(2, 0, 1) - at(2, 0, -1),
                        at(1, 0, 2) - here,
                        at(1, 1, 1) - at(1, 1, -1),
                    ),
                    (
                        ahead_x - at(0),
                        at(3) - here,
                        at(2, 0, 1) - at(0, 0, 1),
                        at(2, 1) - at(0, 1),
                    ),
                )
                crossing = jnp.zeros((8, LANES), F32)
                for i in range(LEVELS):
                    minus = levels[i] - here
                    size = jnp.abs(minus)
                    own = None
                    terms = []
                    for ahead in (ahead_x, ahead_y, ahead_z):
                        upper = ahead - levels[i]
                        w = jnp.maximum(0.0, minus * upper)
                        crossing = crossing + w
                        part = w * jnp.abs(upper)
                        own = part if own is None else own + part
                        terms.append(w * size)
                    for m in range(3):
                        g = grads[m]
                        sums[i * 3 + m] = sums[i * 3 + m] + (
                            (own * g[0] + terms[0] * g[1]) + (terms[1] * g[2] + terms[2] * g[3])
                        )
                cells[half * BRICK + strip * 8 : half * BRICK + strip * 8 + 8, :] = crossing
            for n in range(LEVELS * 3):
                acc[half, pl.ds(pl.multiple_of((n * depth + z) * 8, 8), 8), :] = sums[n]
        quad = iota((height // 4, LANES), 1) // BRICK
        t = [cells[pl.ds(b, height // 4, stride=4), :] for b in range(4)]
        u = [None] * 4
        for b in range(2):
            u[b] = jnp.where(quad < 2, t[b], pltpu.roll(t[b + 2], 64, 1))
            u[b + 2] = jnp.where(quad < 2, pltpu.roll(t[b], 64, 1), t[b + 2])
        even = quad % 2 == 0
        for b in (0, 2):
            o0 = jnp.where(even, u[b], pltpu.roll(u[b + 1], 32, 1))
            o1 = jnp.where(even, pltpu.roll(u[b], 96, 1), u[b + 1])
            for half in range(2):
                at_rows = pl.ds(pl.multiple_of(z * 8, 8), 8)
                bricks[half * 4 + b, at_rows, :] = o0[half * 8 : half * 8 + 8]
                bricks[half * 4 + b + 1, at_rows, :] = o1[half * 8 : half * 8 + 8]

    picks = []
    for k in range(cols_n):
        target = lax.rem(c + k, cols_n)
        brick = jnp.int32(0)
        found = jnp.int32(0)
        for t in range(active.shape[1]):
            hit = jnp.logical_and(owner[0, t] == target, active[0, t] >= 0)
            brick = jnp.where(hit, active[0, t], brick)
            found = jnp.where(hit, 1, found)
        picks.append((brick, found))

    def copy_of(k, chunk, start, count):
        rows = pl.ds(start, count)
        return pltpu.make_async_remote_copy(
            src_ref=send.at[k, rows, :], dst_ref=recv.at[c, rows, :],
            send_sem=a_send.at[k, chunk], recv_sem=a_recv.at[k, chunk],
            device_id=(r, lax.rem(c + k, cols_n)), device_id_type=MESH,
        )

    chunks = depth // CH
    crows = CH * 8

    def one_chunk(chunk, carry):
        def one_layer(z, inner):
            layer(chunk * CH + z)
            return inner

        lax.fori_loop(0, CH, one_layer, 0)
        start = pl.multiple_of(chunk * crows, crows)
        rows = pl.ds(start, crows)
        for k in range(1, cols_n):
            send[k, rows, :] = bricks[picks[k][0], rows, :]
            copy_of(k, chunk, start, crows).start()
        recv[c, rows, :] = bricks[picks[0][0], rows, :]
        return carry

    lax.fori_loop(0, chunks, one_chunk, 0)

    pick = (iota((8, LANES), 1) // BRICK == iota((8, LANES), 0)).astype(F32)
    wide = acc.shape[1] // 8
    for half in range(2):
        total = acc[half, pl.ds(0, wide, stride=8), :]
        for s in range(1, 8):
            total = total + acc[half, pl.ds(s, wide, stride=8), :]
        out = lax.dot_general(
            pick, total, (((1,), (1,)), ((), ())),
            precision=lax.Precision.HIGHEST, preferred_element_type=F32,
        ) * (1.0 / 32.0)
        for b in range(4):
            for part in range(wide // LANES):
                nrm[half * 4 + b, part : part + 1, :] = out[
                    b : b + 1, part * LANES : (part + 1) * LANES
                ]
    flag_row = iota((8, LANES), 0) == 3
    base = chunks * crows
    for k in range(cols_n):
        brick, found = picks[k]
        tail = jnp.where(flag_row, found.astype(F32), nrm[brick])
        if k:
            send[k, base : base + 8, :] = tail
            copy_of(k, chunks, base, 8).start()
        else:
            recv[c, base : base + 8, :] = tail

    for k in range(1, cols_n):
        for chunk in range(chunks):
            copy_of(k, chunk, chunk * crows, crows).wait()
        copy_of(k, chunks, base, 8).wait()


def place(recv, crossing, normals):
    sources = recv.shape[0]
    rows = recv.shape[1] - 8
    slots = crossing.shape[1]
    count = jnp.int32(0)
    index = [jnp.int32(0)] * slots
    filled = [jnp.int32(0)] * slots
    for s in range(sources):
        flag = jnp.max(recv[s, rows + 3 : rows + 4, :]) > 0.5
        for n in range(slots):
            hit = jnp.logical_and(flag, count == n)
            index[n] = jnp.where(hit, s, index[n])
            filled[n] = jnp.where(hit, 1, filled[n])
        count = count + flag.astype(jnp.int32)

    def block(i, carry):
        start = pl.multiple_of(i * 8, 8)
        for n in range(slots):
            v = recv[index[n], pl.ds(start, 8), :]
            v = jnp.where(filled[n] > 0, v, 0.0)
            for s in range(8):
                at = pl.ds(pl.multiple_of((start + s) * LANES, LANES), LANES)
                crossing[0, n : n + 1, at] = v[s : s + 1, :]
        return carry

    lax.fori_loop(0, rows // 8, block, 0)
    for n in range(slots):
        v = jnp.where(filled[n] > 0, recv[index[n], rows : rows + 8, :], 0.0)
        length = normals.shape[2]
        for p in range(0, length, LANES):
            width = min(LANES, length - p)
            normals[0, n : n + 1, p : p + width] = v[p // LANES : p // LANES + 1, :width]


def shards(rows_n, cols_n, density, active, owner_map, isovalues):
    depth, height, width = density.shape
    ext = height + 16
    local = active.shape[1]
    chunks = depth // CH
    vmem = pl.BlockSpec(memory_space=pltpu.VMEM)
    smem = pl.BlockSpec(memory_space=pltpu.SMEM)
    smoothed, received = pl.pallas_call(
        functools.partial(kernel, rows_n, cols_n),
        out_shape=(
            jax.ShapeDtypeStruct(density.shape, F32),
            jax.ShapeDtypeStruct((cols_n, PAY, LANES), F32),
        ),
        in_specs=[vmem, smem, smem, smem],
        out_specs=(vmem, vmem),
        scratch_shapes=[
            pltpu.VMEM((depth + 4, ext, LANES), F32),
            pltpu.VMEM((ext, LANES), F32),
            pltpu.VMEM((ext, LANES), F32),
            pltpu.VMEM((height, LANES), F32),
            pltpu.VMEM((height, LANES), F32),
            pltpu.VMEM((4, depth + 3, ext, LANES), F32),
            pltpu.VMEM((2 * LANES, 4 * LANES), jnp.bfloat16),
            pltpu.VMEM((height, LANES), F32),
            pltpu.VMEM((local, depth * 8, LANES), F32),
            pltpu.VMEM((local, 8, LANES), F32),
            pltpu.VMEM((2, 384 * 8, LANES), F32),
            pltpu.VMEM((cols_n, PAY, LANES), F32),
            pltpu.SemaphoreType.DMA((8,)),
            pltpu.SemaphoreType.DMA((8,)),
            pltpu.SemaphoreType.DMA((cols_n, chunks + 1)),
            pltpu.SemaphoreType.DMA((cols_n, chunks + 1)),
        ],
        compiler_params=pltpu.CompilerParams(
            collective_id=0, has_side_effects=True, vmem_limit_bytes=48 << 20
        ),
        name="halo_surface_exchange",
    )(density, active, owner_map, isovalues)
    quarter = local // 4
    capacity = (local + (cols_n - 1) * quarter + cols_n - 1) // cols_n
    crossing, normals = pl.pallas_call(
        place,
        out_shape=(
            jax.ShapeDtypeStruct((1, capacity, depth * BRICK * BRICK), F32),
            jax.ShapeDtypeStruct((1, capacity, LEVELS * 3 * depth), F32),
        ),
        in_specs=[vmem],
        out_specs=(vmem, vmem),
        compiler_params=pltpu.CompilerParams(vmem_limit_bytes=32 << 20),
        name="place_slots",
    )(received)
    return smoothed, crossing, normals


def solution(mesh):
    placed = (P(None, "row", "col"), P("row", "col"), P("row", "col"), P())
    return jax.shard_map(
        functools.partial(shards, mesh.shape["row"], mesh.shape["col"]),
        mesh=mesh,
        in_specs=placed,
        out_specs=(P(None, "row", "col"), P("row", "col", None), P("row", "col", None)),
        check_vma=False,
    )
```

```python
import functools

import jax
import jax.numpy as jnp
from jax import lax
from jax.experimental import pallas as pl
from jax.experimental.pallas import tpu as pltpu
from jax.sharding import PartitionSpec as P

BRICK = 32
LEVELS = 3
LANES = 128
PAY = 264
CH = 4
MESH = pl.DeviceIdType.MESH
F32 = jnp.float32
DIRS = ((-1, 0), (1, 0), (0, -1), (0, 1), (-1, -1), (-1, 1), (1, -1), (1, 1))


def iota(shape, dim):
    return lax.broadcasted_iota(jnp.int32, shape, dim)


def five(far, near, mid):
    return 10.0 * mid + 4.0 * near - far


def kernel(
    rows_n, cols_n, dens, active_in, owner_in, iso_in,
    smooth, recv,
    dext, side_l, side_r, pack_l, pack_r, pack_y, side_y, shifted, wmat, lhs, cells, bricks, nrm,
    acc, send, active, owner, iso,
    in_sem, hs_send, hs_recv, a_send, a_recv,
):
    depth = dens.shape[0]
    height = dens.shape[1]
    ext = height + 16
    r = lax.axis_index("row")
    c = lax.axis_index("col")
    up, down = r > 0, r < rows_n - 1
    left, right = c > 0, c < cols_n - 1

    def exists(dy, dx):
        ok = None
        for d, lo, hi in ((dy, up, down), (dx, left, right)):
            if d:
                e = lo if d < 0 else hi
                ok = e if ok is None else jnp.logical_and(ok, e)
        return ok

    layers = pl.ds(2, depth)
    loads = [
        pltpu.make_async_copy(src, dst, in_sem.at[n])
        for n, (src, dst) in enumerate(
            (
                (dens, dext.at[layers, pl.ds(8, height), :]),
                (active_in, active),
                (owner_in, owner),
                (iso_in, iso),
            )
        )
    ]
    for load in loads:
        load.start()
    barrier = pltpu.get_barrier_semaphore()
    for dy, dx in DIRS:
        if dy:
            @pl.when(exists(dy, dx))
            def _():
                pl.semaphore_signal(barrier, inc=1, device_id=(r + dy, c + dx), device_id_type=MESH)
    for k in range(1, cols_n):
        pl.semaphore_signal(
            barrier, inc=1, device_id=(r, lax.rem(c + k, cols_n)), device_id_type=MESH
        )

    lane = iota((height, LANES), 1)
    group = lane // 4

    def pack(z, carry):
        first, last = carry
        rolled = pltpu.roll(dext[z + 2, 8 : 8 + height, :], 4 * z, 1)
        first = jnp.where(group == z, rolled, first)
        last = jnp.where(group == (z + depth - 1) % depth, rolled, last)
        return first, last

    upper_half = iota((8, LANES), 0) < 4

    def pack_rows(pair, carry):
        z = 2 * pair + 2
        at_rows = pl.ds(pl.multiple_of(pair * 8, 8), 8)
        pack_y[0, at_rows, :] = jnp.where(
            upper_half, dext[z, 8:16, :], pltpu.roll(dext[z + 1, 8:16, :], 4, 0)
        )
        pack_y[1, at_rows, :] = jnp.where(
            upper_half,
            pltpu.roll(dext[z, height : height + 8, :], 4, 0),
            dext[z + 1, height : height + 8, :],
        )
        return carry

    zero = jnp.zeros((height, LANES), F32)
    loads[0].wait()
    lax.fori_loop(0, depth // 2, pack_rows, 0, unroll=4)
    first, last = lax.fori_loop(0, depth, pack, (zero, zero), unroll=4)
    pack_l[...] = first
    pack_r[...] = last

    n_wait = (cols_n - 1) + (up.astype(jnp.int32) + down.astype(jnp.int32)) * (
        1 + left.astype(jnp.int32) + right.astype(jnp.int32)
    )
    pl.semaphore_wait(barrier, n_wait)

    top, body, bottom = pl.ds(0, 8), pl.ds(8, height), pl.ds(8 + height, 8)
    inner_top, inner_bottom = pl.ds(0, 8), pl.ds(height - 8, 8)
    plans = {
        (-1, 0): (pack_y.at[0], side_y.at[1]),
        (1, 0): (pack_y.at[1], side_y.at[0]),
        (0, -1): (pack_l, side_r.at[body, :]),
        (0, 1): (pack_r, side_l.at[body, :]),
        (-1, -1): (pack_l.at[inner_top, :], side_r.at[bottom, :]),
        (-1, 1): (pack_r.at[inner_top, :], side_l.at[bottom, :]),
        (1, -1): (pack_l.at[inner_bottom, :], side_r.at[top, :]),
        (1, 1): (pack_r.at[inner_bottom, :], side_l.at[top, :]),
    }
    halo = []
    for n, (dy, dx) in enumerate(DIRS):
        src, dst = plans[(dy, dx)]
        copy = pltpu.make_async_remote_copy(
            src_ref=src, dst_ref=dst, send_sem=hs_send.at[n], recv_sem=hs_recv.at[n],
            device_id=(r + dy, c + dx), device_id_type=MESH,
        )
        halo.append(copy)

        @pl.when(exists(dy, dx))
        def _():
            copy.start()

    for dy, dx in DIRS:
        @pl.when(jnp.logical_not(exists(-dy, -dx)))
        def _():
            dst = plans[(dy, dx)][1]
            dst[...] = jnp.zeros(dst.shape, F32)
    plane0 = jnp.zeros((ext, LANES), F32)
    for z in (0, 1, depth + 2, depth + 3):
        dext[z] = plane0
    for q in range(4):
        for z in (0, depth + 1, depth + 2):
            shifted[q, z] = plane0

    k_id = iota((2 * LANES, LANES), 0)
    n_id = iota((2 * LANES, LANES), 1)
    k_col = jnp.where(k_id < LANES + LANES // 2, k_id, k_id - 2 * LANES)
    for q in range(4):
        col = n_id + (q - 1)
        gap = jnp.abs(k_col - col)
        tap = jnp.where(gap == 0, 10.0, jnp.where(gap == 1, 4.0, jnp.where(gap == 2, -1.0, 0.0)))
        inside = ((col >= 0) | left) & ((col < LANES) | right)
        band = jnp.where(inside, tap * (1.0 / 4096.0), 0.0).astype(jnp.bfloat16)
        for part in range(2):
            wmat[part * 2 * LANES : (part + 1) * 2 * LANES, q * LANES : (q + 1) * LANES] = band
    for b in range(2):
        acc[b, LEVELS * 3 * depth * 8 :, :] = jnp.zeros(
            (acc.shape[1] - LEVELS * 3 * depth * 8, LANES), F32
        )

    for n, (dy, dx) in enumerate(DIRS):
        @pl.when(exists(-dy, -dx))
        def _():
            halo[n].wait_recv()
    for load in loads[1:]:
        load.wait()

    def unpack_rows(pair, carry):
        z = 2 * pair + 2
        at_rows = pl.ds(pl.multiple_of(pair * 8, 8), 8)
        above, below = side_y[0, at_rows, :], side_y[1, at_rows, :]
        dext[z, 0:8, :] = pltpu.roll(above, 4, 0)
        dext[z + 1, 0:8, :] = above
        dext[z, 8 + height :, :] = below
        dext[z + 1, 8 + height :, :] = pltpu.roll(below, 4, 0)
        return carry

    lax.fori_loop(0, depth // 2, unpack_rows, 0, unroll=4)

    row_id = iota((ext, LANES), 0)
    lane_id = iota((ext, LANES), 1)
    in_rows = ((row_id >= 8) | up) & ((row_id < 8 + height) | down)

    def along_y(v):
        return five(
            pltpu.roll(v, 2, 0) + pltpu.roll(v, ext - 2, 0),
            pltpu.roll(v, 1, 0) + pltpu.roll(v, ext - 1, 0),
            v,
        )

    def side_filter(v):
        def moved(k):
            if k > 0:
                return jnp.where(lane_id < LANES - 4 * k, pltpu.roll(v, LANES - 4 * k, 1), 0.0)
            return jnp.where(lane_id >= -4 * k, pltpu.roll(v, -4 * k, 1), 0.0)

        out = along_y(five(moved(-2) + moved(2), moved(-1) + moved(1), v))
        return jnp.where(in_rows, out, 0.0)

    side_r[...] = side_filter(side_r[...])
    side_l[...] = pltpu.roll(side_filter(pltpu.roll(side_l[...], 4, 1)), LANES - 4, 1)

    def filter_chunk(chunk):
        for i in range(CH):
            z = chunk * CH + i
            v = [dext[z + n] for n in range(5)]
            main = along_y(five(v[0] + v[4], v[1] + v[3], v[2]))
            main = jnp.where(in_rows, main, 0.0)
            back = (LANES - 4 * z) % LANES
            edge = jnp.where(
                lane_id < 4,
                pltpu.roll(side_r[...], back, 1),
                jnp.where(lane_id >= LANES - 4, pltpu.roll(side_l[...], back, 1), 0.0),
            )
            for n, part in enumerate((main, edge)):
                high = part.astype(jnp.bfloat16)
                low = (part - high.astype(F32)).astype(jnp.bfloat16)
                rows = slice(i * ext, (i + 1) * ext)
                lhs[rows, n * LANES : (n + 1) * LANES] = high
                lhs[rows, (n + 2) * LANES : (n + 3) * LANES] = low
        out = jnp.dot(lhs[...], wmat[...], preferred_element_type=F32)
        for i in range(CH):
            z = chunk * CH + i
            for q in range(4):
                shifted[q, z + 1] = out[i * ext : (i + 1) * ext, q * LANES : (q + 1) * LANES]
            smooth[z] = out[i * ext + 8 : i * ext + 8 + height, LANES : 2 * LANES]

    levels = [iso[i] for i in range(LEVELS)]

    def layer(z):
        for half in range(2):
            sums = [jnp.zeros((8, LANES), F32)] * (LEVELS * 3)
            for strip in range(4):
                base = 8 + half * BRICK + strip * 8

                def at(q, dz=0, dy=0):
                    return shifted[q, z + 1 + dz, pl.ds(base + dy, 8), :]

                here, ahead_x = at(1), at(2)
                ahead_y, ahead_z = at(1, 0, 1), at(1, 1)
                back_z = at(1, -1)
                grads = (
                    (
                        ahead_z - back_z,
                        at(2, 1) - at(2, -1),
                        at(1, 1, 1) - at(1, -1, 1),
                        at(1, 2) - here,
                    ),
                    (
                        ahead_y - at(1, 0, -1),
                        at(2, 0, 1) - at(2, 0, -1),
                        at(1, 0, 2) - here,
                        at(1, 1, 1) - at(1, 1, -1),
                    ),
                    (
                        ahead_x - at(0),
                        at(3) - here,
                        at(2, 0, 1) - at(0, 0, 1),
                        at(2, 1) - at(0, 1),
                    ),
                )
                crossing = jnp.zeros((8, LANES), F32)
                for i in range(LEVELS):
                    minus = levels[i] - here
                    size = jnp.abs(minus)
                    own = None
                    terms = []
                    for ahead in (ahead_x, ahead_y, ahead_z):
                        upper = ahead - levels[i]
                        w = jnp.maximum(0.0, minus * upper)
                        crossing = crossing + w
                        part = w * jnp.abs(upper)
                        own = part if own is None else own + part
                        terms.append(w * size)
                    for m in range(3):
                        g = grads[m]
                        sums[i * 3 + m] = sums[i * 3 + m] + (
                            (own * g[0] + terms[0] * g[1]) + (terms[1] * g[2] + terms[2] * g[3])
                        )
                cells[half * BRICK + strip * 8 : half * BRICK + strip * 8 + 8, :] = crossing
            for n in range(LEVELS * 3):
                acc[half, pl.ds(pl.multiple_of((n * depth + z) * 8, 8), 8), :] = sums[n]
        quad = iota((height // 4, LANES), 1) // BRICK
        t = [cells[pl.ds(b, height // 4, stride=4), :] for b in range(4)]
        u = [None] * 4
        for b in range(2):
            u[b] = jnp.where(quad < 2, t[b], pltpu.roll(t[b + 2], 64, 1))
            u[b + 2] = jnp.where(quad < 2, pltpu.roll(t[b], 64, 1), t[b + 2])
        even = quad % 2 == 0
        for b in (0, 2):
            o0 = jnp.where(even, u[b], pltpu.roll(u[b + 1], 32, 1))
            o1 = jnp.where(even, pltpu.roll(u[b], 96, 1), u[b + 1])
            for half in range(2):
                at_rows = pl.ds(pl.multiple_of(z * 8, 8), 8)
                bricks[half * 4 + b, at_rows, :] = o0[half * 8 : half * 8 + 8]
                bricks[half * 4 + b + 1, at_rows, :] = o1[half * 8 : half * 8 + 8]

    picks = []
    for k in range(cols_n):
        target = lax.rem(c + k, cols_n)
        brick = jnp.int32(0)
        found = jnp.int32(0)
        for t in range(active.shape[1]):
            hit = jnp.logical_and(owner[0, t] == target, active[0, t] >= 0)
            brick = jnp.where(hit, active[0, t], brick)
            found = jnp.where(hit, 1, found)
        picks.append((brick, found))

    def copy_of(k, chunk, start, count):
        rows = pl.ds(start, count)
        return pltpu.make_async_remote_copy(
            src_ref=send.at[k, rows, :], dst_ref=recv.at[c, rows, :],
            send_sem=a_send.at[k, chunk], recv_sem=a_recv.at[k, chunk],
            device_id=(r, lax.rem(c + k, cols_n)), device_id_type=MESH,
        )

    chunks = depth // CH
    crows = CH * 8

    def one_chunk(chunk, carry):
        @pl.when(chunk + 1 < chunks)
        def _():
            filter_chunk(chunk + 1)

        def one_layer(z, inner):
            layer(chunk * CH + z)
            return inner

        lax.fori_loop(0, CH, one_layer, 0, unroll=2)
        start = pl.multiple_of(chunk * crows, crows)
        rows = pl.ds(start, crows)
        for k in range(1, cols_n):
            send[k, rows, :] = bricks[picks[k][0], rows, :]
            copy_of(k, chunk, start, crows).start()
        recv[c, rows, :] = bricks[picks[0][0], rows, :]
        return carry

    filter_chunk(0)
    lax.fori_loop(0, chunks, one_chunk, 0)

    pick = (iota((8, LANES), 1) // BRICK == iota((8, LANES), 0)).astype(F32)
    wide = acc.shape[1] // 8
    for half in range(2):
        total = acc[half, pl.ds(0, wide, stride=8), :]
        for s in range(1, 8):
            total = total + acc[half, pl.ds(s, wide, stride=8), :]
        out = lax.dot_general(
            pick, total, (((1,), (1,)), ((), ())),
            precision=lax.Precision.HIGHEST, preferred_element_type=F32,
        ) * (1.0 / 32.0)
        for b in range(4):
            for part in range(wide // LANES):
                nrm[half * 4 + b, part : part + 1, :] = out[
                    b : b + 1, part * LANES : (part + 1) * LANES
                ]
    flag_row = iota((8, LANES), 0) == 3
    base = chunks * crows
    for k in range(cols_n):
        brick, found = picks[k]
        tail = jnp.where(flag_row, found.astype(F32), nrm[brick])
        if k:
            send[k, base : base + 8, :] = tail
            copy_of(k, chunks, base, 8).start()
        else:
            recv[c, base : base + 8, :] = tail

    for k in range(1, cols_n):
        for chunk in range(chunks):
            copy_of(k, chunk, chunk * crows, crows).wait()
        copy_of(k, chunks, base, 8).wait()
    for n, (dy, dx) in enumerate(DIRS):
        @pl.when(exists(dy, dx))
        def _():
            halo[n].wait_send()


def place(smooth_in, recv, smooth, crossing, normals, empty, vectors, sems):
    keep = pltpu.make_async_copy(smooth_in, smooth, sems.at[0])
    keep.start()
    sources = recv.shape[0]
    rows = recv.shape[1] - 8
    slots = crossing.shape[0]
    empty[...] = jnp.zeros(empty.shape, F32)
    count = jnp.int32(0)
    index = [jnp.int32(0)] * slots
    filled = [jnp.int32(0)] * slots
    for s in range(sources):
        flag = jnp.max(recv[s, rows + 3 : rows + 4, :]) > 0.5
        for n in range(slots):
            hit = jnp.logical_and(flag, count == n)
            index[n] = jnp.where(hit, s, index[n])
            filled[n] = jnp.where(hit, 1, filled[n])
        count = count + flag.astype(jnp.int32)
    copies = []
    for n in range(slots):
        copy = pltpu.make_async_copy(
            recv.at[index[n], pl.ds(0, rows), :], crossing.at[n], sems.at[2 + n]
        )
        none = pltpu.make_async_copy(empty, crossing.at[n], sems.at[2 + n])
        copies.append(none)
        pl.when(filled[n] > 0)(copy.start)
        pl.when(filled[n] == 0)(none.start)
    length = normals.shape[2]
    for n in range(slots):
        v = jnp.where(filled[n] > 0, recv[index[n], rows : rows + 8, :], 0.0)
        for p in range(0, length, LANES):
            width = min(LANES, length - p)
            vectors[n, :, p : p + width] = v[p // LANES : p // LANES + 1, :width]
    last = pltpu.make_async_copy(vectors, normals, sems.at[1])
    last.start()
    for copy in copies:
        copy.wait()
    last.wait()
    keep.wait()


def shards(rows_n, cols_n, density, active, owner_map, isovalues):
    depth, height, width = density.shape
    ext = height + 16
    local = active.shape[1]
    chunks = depth // CH
    vmem = pl.BlockSpec(memory_space=pltpu.VMEM)
    hbm = pl.BlockSpec(memory_space=pltpu.HBM)
    anywhere = pl.BlockSpec(memory_space=pl.ANY)
    smoothed, received = pl.pallas_call(
        functools.partial(kernel, rows_n, cols_n),
        out_shape=(
            jax.ShapeDtypeStruct(density.shape, F32),
            jax.ShapeDtypeStruct((cols_n, PAY, LANES), F32),
        ),
        in_specs=[hbm] * 4,
        out_specs=(vmem, vmem),
        scratch_shapes=[
            pltpu.VMEM((depth + 4, ext, LANES), F32),
            pltpu.VMEM((ext, LANES), F32),
            pltpu.VMEM((ext, LANES), F32),
            pltpu.VMEM((height, LANES), F32),
            pltpu.VMEM((height, LANES), F32),
            pltpu.VMEM((2, 4 * depth, LANES), F32),
            pltpu.VMEM((2, 4 * depth, LANES), F32),
            pltpu.VMEM((4, depth + 3, ext, LANES), F32),
            pltpu.VMEM((4 * LANES, 4 * LANES), jnp.bfloat16),
            pltpu.VMEM((CH * ext, 4 * LANES), jnp.bfloat16),
            pltpu.VMEM((height, LANES), F32),
            pltpu.VMEM((local, depth * 8, LANES), F32),
            pltpu.VMEM((local, 8, LANES), F32),
            pltpu.VMEM((2, 384 * 8, LANES), F32),
            pltpu.VMEM((cols_n, PAY, LANES), F32),
            pltpu.SMEM(active.shape, jnp.int32),
            pltpu.SMEM(owner_map.shape, jnp.int32),
            pltpu.SMEM(isovalues.shape, F32),
            pltpu.SemaphoreType.DMA((4,)),
            pltpu.SemaphoreType.DMA((8,)),
            pltpu.SemaphoreType.DMA((8,)),
            pltpu.SemaphoreType.DMA((cols_n, chunks + 1)),
            pltpu.SemaphoreType.DMA((cols_n, chunks + 1)),
        ],
        compiler_params=pltpu.CompilerParams(
            collective_id=0, has_side_effects=True, vmem_limit_bytes=48 << 20
        ),
        name="halo_surface_exchange",
    )(density, active, owner_map, isovalues)
    quarter = local // 4
    capacity = (local + (cols_n - 1) * quarter + cols_n - 1) // cols_n
    cells = depth * BRICK * BRICK
    length = LEVELS * 3 * depth
    smoothed, crossing, normals = pl.pallas_call(
        place,
        out_shape=(
            jax.ShapeDtypeStruct(density.shape, F32),
            jax.ShapeDtypeStruct((capacity, cells // LANES, LANES), F32),
            jax.ShapeDtypeStruct((capacity, 1, length), F32),
        ),
        in_specs=[anywhere, vmem],
        out_specs=(hbm, hbm, hbm),
        scratch_shapes=[
            pltpu.VMEM((cells // LANES, LANES), F32),
            pltpu.VMEM((capacity, 1, length), F32),
            pltpu.SemaphoreType.DMA((2 + capacity,)),
        ],
        compiler_params=pltpu.CompilerParams(vmem_limit_bytes=32 << 20),
        name="place_slots",
    )(smoothed, received)
    return smoothed, crossing.reshape(1, capacity, cells), normals.reshape(1, capacity, length)


def solution(mesh):
    placed = (P(None, "row", "col"), P("row", "col"), P("row", "col"), P())
    return jax.shard_map(
        functools.partial(shards, mesh.shape["row"], mesh.shape["col"]),
        mesh=mesh,
        in_specs=placed,
        out_specs=(P(None, "row", "col"), P("row", "col", None), P("row", "col", None)),
        check_vma=False,
    )
```

```python
import functools

import jax
import jax.numpy as jnp
from jax import lax
from jax.experimental import pallas as pl
from jax.experimental.pallas import tpu as pltpu
from jax.sharding import PartitionSpec as P

BRICK = 32
LEVELS = 3
LANES = 128
PAY = 264
CH = 4
MESH = pl.DeviceIdType.MESH
F32 = jnp.float32
DIRS = ((-1, 0), (1, 0), (0, -1), (0, 1), (-1, -1), (-1, 1), (1, -1), (1, 1))


def iota(shape, dim):
    return lax.broadcasted_iota(jnp.int32, shape, dim)


def five(far, near, mid):
    return 10.0 * mid + 4.0 * near - far


def kernel(
    rows_n, cols_n, dens, codes_in, iso_in,
    smooth, recv,
    dext, side_l, side_r, pack_l, pack_r, pack_y, side_y, shifted, wmat, lhs, cells, bricks, nrm,
    acc, send, inner, codes, iso,
    in_sem, hs_send, hs_recv, a_send, a_recv,
):
    depth = dens.shape[0]
    height = dens.shape[1]
    ext = height + 16
    r = lax.axis_index("row")
    c = lax.axis_index("col")
    up, down = r > 0, r < rows_n - 1
    left, right = c > 0, c < cols_n - 1

    def exists(dy, dx):
        ok = None
        for d, lo, hi in ((dy, up, down), (dx, left, right)):
            if d:
                e = lo if d < 0 else hi
                ok = e if ok is None else jnp.logical_and(ok, e)
        return ok

    layers = pl.ds(2, depth)
    loads = [
        pltpu.make_async_copy(src, dst, in_sem.at[n])
        for n, (src, dst) in enumerate(
            (
                (dens, dext.at[layers, pl.ds(8, height), :]),
                (codes_in, codes),
                (iso_in, iso),
            )
        )
    ]
    for load in loads:
        load.start()
    barrier = pltpu.get_barrier_semaphore()
    for dy, dx in DIRS:
        if dy:
            @pl.when(exists(dy, dx))
            def _():
                pl.semaphore_signal(barrier, inc=1, device_id=(r + dy, c + dx), device_id_type=MESH)
    for k in range(1, cols_n):
        pl.semaphore_signal(
            barrier, inc=1, device_id=(r, lax.rem(c + k, cols_n)), device_id_type=MESH
        )

    lane = iota((height, LANES), 1)
    group = lane // 4

    def pack(z, carry):
        first, last = carry
        rolled = pltpu.roll(dext[z + 2, 8 : 8 + height, :], 4 * z, 1)
        first = jnp.where(group == z, rolled, first)
        last = jnp.where(group == (z + depth - 1) % depth, rolled, last)
        return first, last

    upper_half = iota((8, LANES), 0) < 4

    def pack_rows(pair, carry):
        z = 2 * pair + 2
        at_rows = pl.ds(pl.multiple_of(pair * 8, 8), 8)
        pack_y[0, at_rows, :] = jnp.where(
            upper_half, dext[z, 8:16, :], pltpu.roll(dext[z + 1, 8:16, :], 4, 0)
        )
        pack_y[1, at_rows, :] = jnp.where(
            upper_half,
            pltpu.roll(dext[z, height : height + 8, :], 4, 0),
            dext[z + 1, height : height + 8, :],
        )
        return carry

    zero = jnp.zeros((height, LANES), F32)
    loads[0].wait()
    lax.fori_loop(0, depth // 2, pack_rows, 0, unroll=4)
    first, last = lax.fori_loop(0, depth, pack, (zero, zero), unroll=4)
    pack_l[...] = first
    pack_r[...] = last

    n_wait = (cols_n - 1) + (up.astype(jnp.int32) + down.astype(jnp.int32)) * (
        1 + left.astype(jnp.int32) + right.astype(jnp.int32)
    )
    pl.semaphore_wait(barrier, n_wait)

    top, body, bottom = pl.ds(0, 8), pl.ds(8, height), pl.ds(8 + height, 8)
    inner_top, inner_bottom = pl.ds(0, 8), pl.ds(height - 8, 8)
    plans = {
        (-1, 0): (pack_y.at[0], side_y.at[1]),
        (1, 0): (pack_y.at[1], side_y.at[0]),
        (0, -1): (pack_l, side_r.at[body, :]),
        (0, 1): (pack_r, side_l.at[body, :]),
        (-1, -1): (pack_l.at[inner_top, :], side_r.at[bottom, :]),
        (-1, 1): (pack_r.at[inner_top, :], side_l.at[bottom, :]),
        (1, -1): (pack_l.at[inner_bottom, :], side_r.at[top, :]),
        (1, 1): (pack_r.at[inner_bottom, :], side_l.at[top, :]),
    }
    halo = []
    for n, (dy, dx) in enumerate(DIRS):
        src, dst = plans[(dy, dx)]
        copy = pltpu.make_async_remote_copy(
            src_ref=src, dst_ref=dst, send_sem=hs_send.at[n], recv_sem=hs_recv.at[n],
            device_id=(r + dy, c + dx), device_id_type=MESH,
        )
        halo.append(copy)

        @pl.when(exists(dy, dx))
        def _():
            copy.start()

    for dy, dx in DIRS:
        @pl.when(jnp.logical_not(exists(-dy, -dx)))
        def _():
            dst = plans[(dy, dx)][1]
            dst[...] = jnp.zeros(dst.shape, F32)
    plane0 = jnp.zeros((ext, LANES), F32)
    for z in (0, 1, depth + 2, depth + 3):
        dext[z] = plane0
    for q in range(4):
        for z in (0, depth + 1, depth + 2):
            shifted[q, z] = plane0

    k_id = iota((2 * LANES, LANES), 0)
    n_id = iota((2 * LANES, LANES), 1)
    k_col = jnp.where(k_id < LANES + LANES // 2, k_id, k_id - 2 * LANES)
    for q in range(4):
        col = n_id + (q - 1)
        gap = jnp.abs(k_col - col)
        tap = jnp.where(gap == 0, 10.0, jnp.where(gap == 1, 4.0, jnp.where(gap == 2, -1.0, 0.0)))
        inside = ((col >= 0) | left) & ((col < LANES) | right)
        band = jnp.where(inside, tap * (1.0 / 4096.0), 0.0).astype(jnp.bfloat16)
        for part in range(2):
            wmat[part * 2 * LANES : (part + 1) * 2 * LANES, q * LANES : (q + 1) * LANES] = band
    for b in range(2):
        acc[b, LEVELS * 3 * depth * 8 :, :] = jnp.zeros(
            (acc.shape[1] - LEVELS * 3 * depth * 8, LANES), F32
        )

    def along_z(z, start, stop):
        v = [dext[z + n, start:stop, :] for n in range(5)]
        return five(v[0] + v[4], v[1] + v[3], v[2])

    def own_layers(z, carry):
        inner[z] = along_z(z, 8, 8 + height)
        return carry

    lax.fori_loop(0, depth, own_layers, 0, unroll=2)

    for n, (dy, dx) in enumerate(DIRS):
        @pl.when(exists(-dy, -dx))
        def _():
            halo[n].wait_recv()
    for load in loads[1:]:
        load.wait()

    def unpack_rows(pair, carry):
        z = 2 * pair + 2
        at_rows = pl.ds(pl.multiple_of(pair * 8, 8), 8)
        above, below = side_y[0, at_rows, :], side_y[1, at_rows, :]
        dext[z, 0:8, :] = pltpu.roll(above, 4, 0)
        dext[z + 1, 0:8, :] = above
        dext[z, 8 + height :, :] = below
        dext[z + 1, 8 + height :, :] = pltpu.roll(below, 4, 0)
        return carry

    lax.fori_loop(0, depth // 2, unpack_rows, 0, unroll=4)

    row_id = iota((ext, LANES), 0)
    lane_id = iota((ext, LANES), 1)
    in_rows = ((row_id >= 8) | up) & ((row_id < 8 + height) | down)

    def along_y(v):
        return five(
            pltpu.roll(v, 2, 0) + pltpu.roll(v, ext - 2, 0),
            pltpu.roll(v, 1, 0) + pltpu.roll(v, ext - 1, 0),
            v,
        )

    def side_filter(v):
        def moved(k):
            if k > 0:
                return jnp.where(lane_id < LANES - 4 * k, pltpu.roll(v, LANES - 4 * k, 1), 0.0)
            return jnp.where(lane_id >= -4 * k, pltpu.roll(v, -4 * k, 1), 0.0)

        out = along_y(five(moved(-2) + moved(2), moved(-1) + moved(1), v))
        return jnp.where(in_rows, out, 0.0)

    side_r[...] = side_filter(side_r[...])
    side_l[...] = pltpu.roll(side_filter(pltpu.roll(side_l[...], 4, 1)), LANES - 4, 1)

    def filter_chunk(chunk):
        for i in range(CH):
            z = chunk * CH + i
            main = along_y(
                jnp.concatenate(
                    [along_z(z, 0, 8), inner[z], along_z(z, 8 + height, ext)], axis=0
                )
            )
            main = jnp.where(in_rows, main, 0.0)
            back = (LANES - 4 * z) % LANES
            edge = jnp.where(
                lane_id < 4,
                pltpu.roll(side_r[...], back, 1),
                jnp.where(lane_id >= LANES - 4, pltpu.roll(side_l[...], back, 1), 0.0),
            )
            for n, part in enumerate((main, edge)):
                high = part.astype(jnp.bfloat16)
                low = (part - high.astype(F32)).astype(jnp.bfloat16)
                rows = slice(i * ext, (i + 1) * ext)
                lhs[rows, n * LANES : (n + 1) * LANES] = high
                lhs[rows, (n + 2) * LANES : (n + 3) * LANES] = low
        out = jnp.dot(lhs[...], wmat[...], preferred_element_type=F32)
        for i in range(CH):
            z = chunk * CH + i
            for q in range(4):
                shifted[q, z + 1] = out[i * ext : (i + 1) * ext, q * LANES : (q + 1) * LANES]
            smooth[z] = out[i * ext + 8 : i * ext + 8 + height, LANES : 2 * LANES]

    levels = [iso[i] for i in range(LEVELS)]

    def layer(z):
        for half in range(2):
            sums = [jnp.zeros((8, LANES), F32)] * (LEVELS * 3)
            for strip in range(4):
                base = 8 + half * BRICK + strip * 8

                def at(q, dz=0, dy=0):
                    return shifted[q, z + 1 + dz, pl.ds(base + dy, 8), :]

                here, ahead_x = at(1), at(2)
                ahead_y, ahead_z = at(1, 0, 1), at(1, 1)
                back_z = at(1, -1)
                grads = (
                    (
                        ahead_z - back_z,
                        at(2, 1) - at(2, -1),
                        at(1, 1, 1) - at(1, -1, 1),
                        at(1, 2) - here,
                    ),
                    (
                        ahead_y - at(1, 0, -1),
                        at(2, 0, 1) - at(2, 0, -1),
                        at(1, 0, 2) - here,
                        at(1, 1, 1) - at(1, 1, -1),
                    ),
                    (
                        ahead_x - at(0),
                        at(3) - here,
                        at(2, 0, 1) - at(0, 0, 1),
                        at(2, 1) - at(0, 1),
                    ),
                )
                crossing = jnp.zeros((8, LANES), F32)
                for i in range(LEVELS):
                    minus = levels[i] - here
                    size = jnp.abs(minus)
                    own = None
                    terms = []
                    for ahead in (ahead_x, ahead_y, ahead_z):
                        upper = ahead - levels[i]
                        w = jnp.maximum(0.0, minus * upper)
                        crossing = crossing + w
                        part = w * jnp.abs(upper)
                        own = part if own is None else own + part
                        terms.append(w * size)
                    for m in range(3):
                        g = grads[m]
                        sums[i * 3 + m] = sums[i * 3 + m] + (
                            (own * g[0] + terms[0] * g[1]) + (terms[1] * g[2] + terms[2] * g[3])
                        )
                cells[half * BRICK + strip * 8 : half * BRICK + strip * 8 + 8, :] = crossing
            for n in range(LEVELS * 3):
                acc[half, pl.ds(pl.multiple_of((n * depth + z) * 8, 8), 8), :] = sums[n]
        quad = iota((height // 4, LANES), 1) // BRICK
        t = [cells[pl.ds(b, height // 4, stride=4), :] for b in range(4)]
        u = [None] * 4
        for b in range(2):
            u[b] = jnp.where(quad < 2, t[b], pltpu.roll(t[b + 2], 64, 1))
            u[b + 2] = jnp.where(quad < 2, pltpu.roll(t[b], 64, 1), t[b + 2])
        even = quad % 2 == 0
        for b in (0, 2):
            o0 = jnp.where(even, u[b], pltpu.roll(u[b + 1], 32, 1))
            o1 = jnp.where(even, pltpu.roll(u[b], 96, 1), u[b + 1])
            for half in range(2):
                at_rows = pl.ds(pl.multiple_of(z * 8, 8), 8)
                bricks[half * 4 + b, at_rows, :] = o0[half * 8 : half * 8 + 8]
                bricks[half * 4 + b + 1, at_rows, :] = o1[half * 8 : half * 8 + 8]

    picks = []
    for k in range(cols_n):
        target = lax.rem(c + k, cols_n)
        brick = jnp.int32(0)
        found = jnp.int32(0)
        for t in range(codes.shape[1]):
            code = codes[0, t]
            hit = jnp.right_shift(code, 8) == target
            brick = jnp.where(hit, jnp.bitwise_and(code, 255), brick)
            found = jnp.where(hit, 1, found)
        picks.append((brick, found))

    def copy_of(k, chunk, start, count):
        rows = pl.ds(start, count)
        return pltpu.make_async_remote_copy(
            src_ref=send.at[k, rows, :], dst_ref=recv.at[c, rows, :],
            send_sem=a_send.at[k, chunk], recv_sem=a_recv.at[k, chunk],
            device_id=(r, lax.rem(c + k, cols_n)), device_id_type=MESH,
        )

    chunks = depth // CH
    crows = CH * 8

    def one_chunk(chunk, carry):
        @pl.when(chunk + 1 < chunks)
        def _():
            filter_chunk(chunk + 1)

        def one_layer(z, inner):
            layer(chunk * CH + z)
            return inner

        lax.fori_loop(0, CH, one_layer, 0, unroll=4)
        start = pl.multiple_of(chunk * crows, crows)
        rows = pl.ds(start, crows)
        for k in range(1, cols_n):
            send[k, rows, :] = bricks[picks[k][0], rows, :]
            copy_of(k, chunk, start, crows).start()
        recv[c, rows, :] = bricks[picks[0][0], rows, :]
        return carry

    filter_chunk(0)
    lax.fori_loop(0, chunks, one_chunk, 0)

    pick = (iota((8, LANES), 1) // BRICK == iota((8, LANES), 0)).astype(F32)
    wide = acc.shape[1] // 8
    for half in range(2):
        total = acc[half, pl.ds(0, wide, stride=8), :]
        for s in range(1, 8):
            total = total + acc[half, pl.ds(s, wide, stride=8), :]
        out = lax.dot_general(
            pick, total, (((1,), (1,)), ((), ())),
            precision=lax.Precision.HIGHEST, preferred_element_type=F32,
        ) * (1.0 / 32.0)
        for b in range(4):
            for part in range(wide // LANES):
                nrm[half * 4 + b, part : part + 1, :] = out[
                    b : b + 1, part * LANES : (part + 1) * LANES
                ]
    flag_row = iota((8, LANES), 0) == 3
    base = chunks * crows
    for k in range(cols_n):
        brick, found = picks[k]
        tail = jnp.where(flag_row, found.astype(F32), nrm[brick])
        if k:
            send[k, base : base + 8, :] = tail
            copy_of(k, chunks, base, 8).start()
        else:
            recv[c, base : base + 8, :] = tail

    for k in range(1, cols_n):
        for chunk in range(chunks):
            copy_of(k, chunk, chunk * crows, crows).wait()
        copy_of(k, chunks, base, 8).wait()
    for n, (dy, dx) in enumerate(DIRS):
        @pl.when(exists(dy, dx))
        def _():
            halo[n].wait_send()


def place(smooth_in, recv, smooth, crossing, normals, empty, vectors, sems):
    keep = pltpu.make_async_copy(smooth_in, smooth, sems.at[0])
    keep.start()
    sources = recv.shape[0]
    rows = recv.shape[1] - 8
    slots = crossing.shape[0]
    empty[...] = jnp.zeros(empty.shape, F32)
    count = jnp.int32(0)
    index = [jnp.int32(0)] * slots
    filled = [jnp.int32(0)] * slots
    for s in range(sources):
        flag = jnp.max(recv[s, rows + 3 : rows + 4, :]) > 0.5
        for n in range(slots):
            hit = jnp.logical_and(flag, count == n)
            index[n] = jnp.where(hit, s, index[n])
            filled[n] = jnp.where(hit, 1, filled[n])
        count = count + flag.astype(jnp.int32)
    copies = []
    for n in range(slots):
        copy = pltpu.make_async_copy(
            recv.at[index[n], pl.ds(0, rows), :], crossing.at[n], sems.at[2 + n]
        )
        none = pltpu.make_async_copy(empty, crossing.at[n], sems.at[2 + n])
        copies.append(none)
        pl.when(filled[n] > 0)(copy.start)
        pl.when(filled[n] == 0)(none.start)
    length = normals.shape[2]
    for n in range(slots):
        v = jnp.where(filled[n] > 0, recv[index[n], rows : rows + 8, :], 0.0)
        for p in range(0, length, LANES):
            width = min(LANES, length - p)
            vectors[n, :, p : p + width] = v[p // LANES : p // LANES + 1, :width]
    last = pltpu.make_async_copy(vectors, normals, sems.at[1])
    last.start()
    for copy in copies:
        copy.wait()
    last.wait()
    keep.wait()


def shards(rows_n, cols_n, density, active, owner_map, isovalues):
    depth, height, width = density.shape
    ext = height + 16
    local = active.shape[1]
    chunks = depth // CH
    vmem = pl.BlockSpec(memory_space=pltpu.VMEM)
    hbm = pl.BlockSpec(memory_space=pltpu.HBM)
    anywhere = pl.BlockSpec(memory_space=pl.ANY)
    codes = jnp.where(active >= 0, owner_map * 256 + active, -1)
    smoothed, received = pl.pallas_call(
        functools.partial(kernel, rows_n, cols_n),
        out_shape=(
            jax.ShapeDtypeStruct(density.shape, F32),
            jax.ShapeDtypeStruct((cols_n, PAY, LANES), F32),
        ),
        in_specs=[hbm] * 3,
        out_specs=(vmem, vmem),
        scratch_shapes=[
            pltpu.VMEM((depth + 4, ext, LANES), F32),
            pltpu.VMEM((ext, LANES), F32),
            pltpu.VMEM((ext, LANES), F32),
            pltpu.VMEM((height, LANES), F32),
            pltpu.VMEM((height, LANES), F32),
            pltpu.VMEM((2, 4 * depth, LANES), F32),
            pltpu.VMEM((2, 4 * depth, LANES), F32),
            pltpu.VMEM((4, depth + 3, ext, LANES), F32),
            pltpu.VMEM((4 * LANES, 4 * LANES), jnp.bfloat16),
            pltpu.VMEM((CH * ext, 4 * LANES), jnp.bfloat16),
            pltpu.VMEM((height, LANES), F32),
            pltpu.VMEM((local, depth * 8, LANES), F32),
            pltpu.VMEM((local, 8, LANES), F32),
            pltpu.VMEM((2, 384 * 8, LANES), F32),
            pltpu.VMEM((cols_n, PAY, LANES), F32),
            pltpu.VMEM(density.shape, F32),
            pltpu.SMEM(active.shape, jnp.int32),
            pltpu.SMEM(isovalues.shape, F32),
            pltpu.SemaphoreType.DMA((3,)),
            pltpu.SemaphoreType.DMA((8,)),
            pltpu.SemaphoreType.DMA((8,)),
            pltpu.SemaphoreType.DMA((cols_n, chunks + 1)),
            pltpu.SemaphoreType.DMA((cols_n, chunks + 1)),
        ],
        compiler_params=pltpu.CompilerParams(
            collective_id=0, has_side_effects=True, vmem_limit_bytes=48 << 20
        ),
        name="halo_surface_exchange",
    )(density, codes, isovalues)
    quarter = local // 4
    capacity = (local + (cols_n - 1) * quarter + cols_n - 1) // cols_n
    cells = depth * BRICK * BRICK
    length = LEVELS * 3 * depth
    smoothed, crossing, normals = pl.pallas_call(
        place,
        out_shape=(
            jax.ShapeDtypeStruct(density.shape, F32),
            jax.ShapeDtypeStruct((capacity, cells // LANES, LANES), F32),
            jax.ShapeDtypeStruct((capacity, 1, length), F32),
        ),
        in_specs=[anywhere, vmem],
        out_specs=(hbm, hbm, hbm),
        scratch_shapes=[
            pltpu.VMEM((cells // LANES, LANES), F32),
            pltpu.VMEM((capacity, 1, length), F32),
            pltpu.SemaphoreType.DMA((2 + capacity,)),
        ],
        compiler_params=pltpu.CompilerParams(vmem_limit_bytes=32 << 20),
        name="place_slots",
    )(smoothed, received)
    return smoothed, crossing.reshape(1, capacity, cells), normals.reshape(1, capacity, length)


def solution(mesh):
    placed = (P(None, "row", "col"), P("row", "col"), P("row", "col"), P())
    return jax.shard_map(
        functools.partial(shards, mesh.shape["row"], mesh.shape["col"]),
        mesh=mesh,
        in_specs=placed,
        out_specs=(P(None, "row", "col"), P("row", "col", None), P("row", "col", None)),
        check_vma=False,
    )
```
